32 devices in a mesh: line: 2 (over x), section: 16 (over z, y, core).
Axes of the slice: x: 2, y: 2, z: 4, core: 2. Of those that a mesh axis runs over, the one named last changes fastest.
Arguments:
- conductivity: float32 [256, 1024], P(('line', 'section')), parts along dimension 0, may hold values from 0.1 to 10
- forward_start: float32 [32, 4, 128, 1024], P('line', None, 'section'), parts along dimension 0, may hold values from -3 to 3
- adjoint_start: float32 [32, 4, 128, 1024], P('line', None, 'section'), parts along dimension 0, may hold values from -3 to 3
- source_cells: int32 [8, 2], P('line'), parts along dimension 0, may hold values from 0 to 131071
- receiver_cells: int32 [64, 2], P('line'), parts along dimension 0, may hold values from 0 to 131071
- observed: float32 [8, 32], P('line'), parts along dimension 0, may hold values from -60 to 60
- wavenumbers: float32 [16], replicated, may hold values from 0.02 to 2
- quadrature_weights: float32 [16], replicated, may hold values from 0.02 to 0.5
- receiver_offsets: float32 [32], replicated, may hold values from 0 to 4
Outputs:
- gradient: float32 [256, 1024], P(('line', 'section')), parts along dimension 0
- predicted: float32 [8, 32], P('line'), parts along dimension 0
- forward_field: float32 [32, 4, 128, 1024], P('line', None, 'section'), parts along dimension 0
The draws below stay inside these ranges and needn't reach their ends.
There are 2 independent parts, one for each index of `line`. The reference program is written for one: setup_inputs(seed, part) draws one part's arguments, and reference() takes and returns one part's arrays. A program takes and returns all parts, laid end to end along the dimension named above; an argument that names none is the same for every part. Nothing has to cross between parts.
All inputs are finite; a program needn't handle non-finite values.
Results may differ from the reference program's by a relative error of at most 0.00002.
Values sent between devices are 32-bit elements; how exact they have to be, the bound alone decides.
A program may use at most 192 MiB of HBM per device.

```python
import math
import jax
import jax.numpy as jnp

NC = 1024
K = 16
S = 4
R = 32
SWEEPS = 3
NX = 128
CELLS = 131072


def set_ends(array, own_key, smallest, largest):
    index_at = [jax.random.randint(jax.random.fold_in(own_key, axis), (), 0, length) for axis, length in enumerate(array.shape)]
    longest = array.shape.index(max(array.shape))
    neighbour = index_at[:longest] + [(index_at[longest] + 1) % array.shape[longest]] + index_at[longest + 1:]
    return array.at[tuple(index_at)].set(smallest).at[tuple(neighbour)].set(largest)


def block_levels(own_key, dims, shards, low, largest):
    def one(dim, parts):
        draws = jax.random.uniform(jax.random.fold_in(jax.random.fold_in(own_key, 6), dim), (parts,), jnp.float32, low / len(shards), largest / len(shards))
        return jnp.repeat(jnp.exp(draws), dims[dim] // parts).reshape((-1,) + (1,) * (len(dims) - dim - 1))

    factor_of = one(*shards[0])
    for cut in shards[1:]:
        factor_of = factor_of * one(*cut)
    return factor_of


def gaussian(rng, dims, deviation, reach, cuts=(), kind=jnp.bfloat16):
    drawn = deviation * jax.random.normal(rng, dims, jnp.float32)
    if cuts:
        drawn = drawn * block_levels(rng, dims, cuts, -0.22, 0.18)
    return jnp.clip(drawn, -reach, reach).astype(kind)


def setup_inputs(seed: int = 0, part: int = 0) -> dict:
    key_list = jax.random.split(jax.random.key(seed), 10)
    own_keys = jax.random.split(jax.random.fold_in(key_list[9], part), 10)
    return {
        "conductivity": jnp.clip(jnp.exp(math.log(10.0) - 4.6051702 * jax.random.uniform(own_keys[0], (NX, NC), jnp.float32) ** block_levels(own_keys[0], (NX, NC), ((0, 16),), -0.2, 0.2)), 0.1, 10.0),
        "forward_start": gaussian(own_keys[1], (K, S, NX, NC), 0.5, 3.0, ((2, 16),), jnp.float32),
        "adjoint_start": gaussian(own_keys[2], (K, S, NX, NC), 0.5, 3.0, ((2, 16),), jnp.float32),
        "source_cells": set_ends(jax.random.randint(own_keys[3], (S, 2), 0, CELLS), jax.random.fold_in(own_keys[3], 1), 0, CELLS - 1).astype(jnp.int32),
        "receiver_cells": set_ends(jax.random.randint(own_keys[4], (R, 2), 0, CELLS), jax.random.fold_in(own_keys[4], 1), 0, CELLS - 1).astype(jnp.int32),
        "observed": gaussian(own_keys[5], (S, R), 10.0, 60.0, (), jnp.float32),
        "wavenumbers": jnp.clip(jnp.exp(jax.random.uniform(key_list[6], (K,), jnp.float32, math.log(0.02), math.log(2.0))), 0.02, 2.0),
        "quadrature_weights": jnp.clip(jnp.exp(jax.random.uniform(key_list[7], (K,), jnp.float32, math.log(0.02), math.log(0.5))), 0.02, 0.5),
        "receiver_offsets": jnp.clip(jax.random.uniform(key_list[8], (R,), jnp.float32, 0.0, 4.0), 0.0, 4.0),
    }


OMEGA = 0.8
CURRENT = 10.0


def smooth_once(field_win, sigma_win, source_win, wave_sq, valid_rows):
    centre = sigma_win[1:-1]
    face_up = 0.5 * (centre + sigma_win[:-2])
    face_down = 0.5 * (centre + sigma_win[2:])
    side_pad = jnp.pad(centre, ((0, 0), (1, 1)))
    face_left = 0.5 * (centre + side_pad[:, :-2])
    face_right = 0.5 * (centre + side_pad[:, 2:])
    diag_terms = (face_up + face_down + face_left + face_right)[None] + wave_sq[:, None, None] * centre[None]
    diag_terms = diag_terms + (1.0 - valid_rows)[None, :, None]
    middle = field_win[:, :, 1:-1]
    cols_pad = jnp.pad(middle, ((0, 0), (0, 0), (0, 0), (1, 1)))
    beside = face_up * field_win[:, :, :-2] + face_down * field_win[:, :, 2:]
    beside = beside + face_left * cols_pad[..., :-2] + face_right * cols_pad[..., 2:]
    updated = (1.0 - OMEGA) * middle + OMEGA * (source_win + beside) / diag_terms[:, None]
    return updated * valid_rows[:, None]


def sweep_all(field, sigma_pad, source, wave_sq, valid_rows):
    for sweep_index in range(SWEEPS):
        padded = jnp.pad(field, ((0, 0), (0, 0), (1, 1), (0, 0)))
        field = smooth_once(padded, sigma_pad, source, wave_sq, valid_rows)
    return field


def reference(conductivity, forward_start, adjoint_start, source_cells, receiver_cells, observed, wavenumbers, quadrature_weights, receiver_offsets):
    dtype_f = conductivity.dtype
    wave_sq = wavenumbers * wavenumbers
    sigma_pad = jnp.pad(conductivity, ((1, 1), (0, 0)))
    valid_rows = jnp.ones((NX,), dtype_f)
    src_index = jnp.arange(S, dtype=jnp.int32)
    src_rows = source_cells // NC
    src_cols = source_cells % NC
    forward_source = jnp.zeros((S, NX, NC), dtype_f)
    forward_source = forward_source.at[src_index, src_rows[:, 0], src_cols[:, 0]].add(CURRENT)
    forward_source = forward_source.at[src_index, src_rows[:, 1], src_cols[:, 1]].add(-CURRENT)
    forward_field = sweep_all(forward_start, sigma_pad, forward_source[None], wave_sq, valid_rows)
    coef = quadrature_weights[:, None] * jnp.cos(wavenumbers[:, None] * receiver_offsets[None, :])
    rec_rows = receiver_cells // NC
    rec_cols = receiver_cells % NC
    at_m = forward_field[:, :, rec_rows[:, 0], rec_cols[:, 0]]
    at_n = forward_field[:, :, rec_rows[:, 1], rec_cols[:, 1]]
    predicted = jnp.sum(coef[:, None, :] * (at_m - at_n), axis=0)
    amplitude = coef[:, None, :] * (predicted - observed)[None]
    adjoint_source = jnp.zeros((K, S, NX, NC), dtype_f)
    adjoint_source = adjoint_source.at[:, :, rec_rows[:, 0], rec_cols[:, 0]].add(amplitude)
    adjoint_source = adjoint_source.at[:, :, rec_rows[:, 1], rec_cols[:, 1]].add(-amplitude)
    adjoint_field = sweep_all(adjoint_start, sigma_pad, adjoint_source, wave_sq, valid_rows)
    zero_row = jnp.zeros((K, S, 1, NC), dtype_f)
    zero_col = jnp.zeros((K, S, NX, 1), dtype_f)
    fwd_row = jnp.concatenate([forward_field[:, :, 1:], zero_row], axis=2) - forward_field
    adj_row = jnp.concatenate([adjoint_field[:, :, 1:], zero_row], axis=2) - adjoint_field
    fwd_col = jnp.concatenate([forward_field[..., 1:], zero_col], axis=3) - forward_field
    adj_col = jnp.concatenate([adjoint_field[..., 1:], zero_col], axis=3) - adjoint_field
    terms = fwd_row * adj_row + fwd_col * adj_col + wave_sq[:, None, None, None] * forward_field * adjoint_field
    gradient = jnp.sum(terms, axis=(0, 1)) / S
    return gradient, predicted, forward_field
```

```python
import functools

import jax
import jax.numpy as jnp
from jax import lax
from jax.experimental import pallas as pl
from jax.experimental.pallas import tpu as pltpu
from jax.sharding import PartitionSpec as P

SWEEPS = 3
OMEGA = 0.8
CURRENT = 10.0
ABOVE = SWEEPS
BELOW = SWEEPS + 1
LANES = 128


def split3(value):
    high = value.astype(jnp.bfloat16)
    rest = value - high.astype(jnp.float32)
    mid = rest.astype(jnp.bfloat16)
    low = (rest - mid.astype(jnp.float32)).astype(jnp.bfloat16)
    return high, mid, low


def kernel(
    count,
    steps,
    sigma_ref,
    fwd_ref,
    adj_ref,
    src_ref,
    rec_ref,
    obs_ref,
    wave_ref,
    quad_ref,
    off_ref,
    grad_ref,
    pred_ref,
    field_ref,
    sig,
    f0,
    a0,
    t1,
    t2,
    b1,
    b2,
    f3,
    a3,
    rd,
    fsrc,
    asrc,
    face_v,
    face_l,
    face_r,
    coef_s,
    wcol_s,
    oh_e,
    oh_t,
    lhs,
    parts,
    sig_send,
    sig_recv,
    up_send,
    up_recv,
    dn_send,
    dn_recv,
    red_send,
    red_recv,
    load_sem,
    store_sem,
):
    rows, cols = sigma_ref.shape
    fields = fwd_ref.shape[0]
    chunks = fields // 8
    wide = rows + 2 * SWEEPS - 1
    me = lax.axis_index("section")
    has_up = me > 0
    has_dn = me < count - 1
    start = me * rows

    def peer(step):
        bit = (me // (1 << step)) % 2
        return me + (1 - 2 * bit) * (1 << step)

    for which, (ref, buf) in enumerate(((fwd_ref, f0), (adj_ref, a0))):
        for j in range(rows):
            pltpu.make_async_copy(
                ref.at[:, j, :], buf.at[ABOVE + j], load_sem.at[which, j]
            ).start()

    @pl.when(jnp.logical_not(has_up))
    def _():
        sig[0:rows, :] = jnp.zeros((rows, cols), jnp.float32)
        f0[0:ABOVE] = jnp.zeros((ABOVE, fields, cols), jnp.float32)
        a0[0:ABOVE] = jnp.zeros((ABOVE, fields, cols), jnp.float32)

    @pl.when(jnp.logical_not(has_dn))
    def _():
        sig[2 * rows : 3 * rows, :] = jnp.zeros((rows, cols), jnp.float32)
        f0[ABOVE + rows :] = jnp.zeros((BELOW, fields, cols), jnp.float32)
        a0[ABOVE + rows :] = jnp.zeros((BELOW, fields, cols), jnp.float32)

    barrier = pltpu.get_barrier_semaphore()

    @pl.when(has_up)
    def _():
        pl.semaphore_signal(barrier, inc=1, device_id={"section": me - 1})

    @pl.when(has_dn)
    def _():
        pl.semaphore_signal(barrier, inc=1, device_id={"section": me + 1})

    for step in range(steps):
        pl.semaphore_signal(barrier, inc=1, device_id={"section": peer(step)})

    beside = 2 - (count - me) // count - (me + 1) // count
    pl.semaphore_wait(barrier, steps + beside)

    def sig_copy(side):
        place = (2 * rows, 0)[side]
        return pltpu.make_async_remote_copy(
            src_ref=sigma_ref,
            dst_ref=sig.at[pl.ds(place, rows)],
            send_sem=sig_send.at[side],
            recv_sem=sig_recv.at[side],
            device_id={"section": (me - 1, me + 1)[side]},
        )

    def up_copy(which, depth):
        ref, buf = ((fwd_ref, f0), (adj_ref, a0))[which]
        return pltpu.make_async_remote_copy(
            src_ref=ref.at[:, depth, :],
            dst_ref=buf.at[ABOVE + rows + depth],
            send_sem=up_send.at[which, depth],
            recv_sem=up_recv.at[which, depth],
            device_id={"section": me - 1},
        )

    def dn_copy(which, depth):
        ref, buf = ((fwd_ref, f0), (adj_ref, a0))[which]
        return pltpu.make_async_remote_copy(
            src_ref=ref.at[:, rows - 1 - depth, :],
            dst_ref=buf.at[ABOVE - 1 - depth],
            send_sem=dn_send.at[which, depth],
            recv_sem=dn_recv.at[which, depth],
            device_id={"section": me + 1},
        )

    order = [(0, d) for d in range(SWEEPS)] + [(1, d) for d in range(SWEEPS)]
    order += [(0, SWEEPS), (1, SWEEPS)]

    @pl.when(has_up)
    def _():
        sig_copy(0).start()
        for which, depth in order:
            up_copy(which, depth).start()

    @pl.when(has_dn)
    def _():
        sig_copy(1).start()
        for which, depth in order:
            if depth < SWEEPS:
                dn_copy(which, depth).start()

    lane = lax.broadcasted_iota(jnp.int32, (1, LANES), 1)
    eye = lax.broadcasted_iota(jnp.int32, (32, 32), 0) == lax.broadcasted_iota(
        jnp.int32, (32, 32), 1
    )
    rec = rec_ref[...].astype(jnp.float32)
    rec_m = jnp.sum(jnp.where(eye, rec[:, 0:1], 0.0), axis=0, keepdims=True)
    rec_n = jnp.sum(jnp.where(eye, rec[:, 1:2], 0.0), axis=0, keepdims=True)
    none = jnp.full((1, LANES - 64), -1.0, jnp.float32)
    cell_f = jnp.concatenate([rec_m, rec_n, none], axis=1)
    cell = cell_f.astype(jnp.int32)
    cell_row = jnp.where(cell < 0, -1000, cell // cols - start)
    cell_col = jnp.where(cell < 0, -1, cell % cols)
    eye_e = lax.broadcasted_iota(jnp.int32, (LANES, LANES), 0) == lax.broadcasted_iota(
        jnp.int32, (LANES, LANES), 1
    )
    col_down = jnp.sum(
        jnp.where(eye_e, cell_col.astype(jnp.float32), 0.0), axis=1, keepdims=True
    ).astype(jnp.int32)
    oh_e[...] = jnp.where(
        lax.broadcasted_iota(jnp.int32, (LANES, cols), 1) == col_down, 1.0, 0.0
    ).astype(jnp.bfloat16)
    oh_t[...] = jnp.where(
        lax.broadcasted_iota(jnp.int32, (cols, LANES), 0) == cell_col, 1.0, 0.0
    ).astype(jnp.bfloat16)

    kk = wave_ref.shape[1]
    srcs = fields // kk
    pick = lax.broadcasted_iota(jnp.int32, (fields, kk), 0) // srcs == lax.broadcasted_iota(
        jnp.int32, (fields, kk), 1
    )
    wave_col = jnp.sum(jnp.where(pick, wave_ref[...], 0.0), axis=1, keepdims=True)
    quad_col = jnp.sum(jnp.where(pick, quad_ref[...], 0.0), axis=1, keepdims=True)
    off = jnp.concatenate([off_ref[...]] * 4, axis=1)
    sign = jnp.where(lane < 32, 1.0, jnp.where(lane < 64, -1.0, 0.0))
    coef_s[...] = quad_col * jnp.cos(wave_col * off) * sign
    wcol_s[...] = jnp.broadcast_to(wave_col * wave_col, (fields, LANES))

    sig[rows : 2 * rows, :] = sigma_ref[...]

    @pl.when(has_dn)
    def _():
        sig_copy(0).wait_recv()

    @pl.when(has_up)
    def _():
        sig_copy(1).wait_recv()

    base = rows - (SWEEPS - 1)
    lane_c = lax.broadcasted_iota(jnp.int32, (8, cols), 1)
    src_a = jnp.concatenate([src_ref[:, 0:1]] * 2, axis=0)
    src_b = jnp.concatenate([src_ref[:, 1:2]] * 2, axis=0)
    for i in range(wide):
        r = i - (SWEEPS - 1)
        centre = jnp.broadcast_to(sig[base + i : base + i + 1, :], (8, cols))
        above = jnp.broadcast_to(sig[base + i - 1 : base + i, :], (8, cols))
        below = jnp.broadcast_to(sig[base + i + 1 : base + i + 2, :], (8, cols))
        v_up = 0.5 * (centre + above)
        v_dn = 0.5 * (centre + below)
        left = jnp.where(lane_c == 0, 0.0, pltpu.roll(centre, 1, 1))
        right = jnp.where(lane_c == cols - 1, 0.0, pltpu.roll(centre, cols - 1, 1))
        h_l = 0.5 * (centre + left)
        h_r = 0.5 * (centre + right)
        face_v[i] = v_up
        if i == wide - 1:
            face_v[i + 1] = v_dn
        face_l[i] = jnp.where(lane_c == 0, 0.0, h_l)
        face_r[i] = jnp.where(lane_c == cols - 1, 0.0, h_r)
        around = v_up + v_dn + h_l + h_r
        flat = (start + r) * cols + lane_c
        fsrc[i] = jnp.where(flat == src_a, CURRENT, 0.0) + jnp.where(flat == src_b, -CURRENT, 0.0)
        inside = jnp.logical_and(start + r >= 0, start + r < count * rows)
        scale = jnp.where(inside, OMEGA, 0.0)
        safe = jnp.where(inside, 0.0, 1.0)

        def fill(c, _, i=i, around=around, centre=centre, scale=scale, safe=safe):
            ks = pl.ds(pl.multiple_of(c * 8, 8), 8)
            w2 = wcol_s[ks, 0:1]
            rd[i, ks, :] = scale / (around + w2 * centre + safe)
            return 0

        lax.fori_loop(0, chunks, fill, 0)

    def update(src, dst, shift, source, r):
        i = r + (SWEEPS - 1)

        def body(c, _):
            ks = pl.ds(pl.multiple_of(c * 8, 8), 8)
            u = src[r + ABOVE, ks, :]
            f = fsrc[i] if source is None else source[i, ks, :]
            acc = f + face_v[i] * src[r + ABOVE - 1, ks, :]
            acc = acc + face_v[i + 1] * src[r + ABOVE + 1, ks, :]
            acc = acc + face_l[i] * pltpu.roll(u, 1, 1)
            acc = acc + face_r[i] * pltpu.roll(u, cols - 1, 1)
            dst[r + shift, ks, :] = (1.0 - OMEGA) * u + acc * rd[i, ks, :]
            return 0

        lax.fori_loop(0, chunks, body, 0)

    def span(level, lo, number, stride):
        src, dst, shift, source = level

        def body(j, _):
            update(src, dst, shift, source, lo + j * stride)
            return 0

        lax.fori_loop(0, number, body, 0)

    def sweeps(which, first, last, source, upto):
        one, two = ((t1, t2), (b1, b2))[which]
        levels = (
            (first, one, ABOVE, source),
            (one, two, ABOVE, source),
            (two, last, 0, source),
        )
        ref, buf = ((fwd_ref, f0), (adj_ref, a0))[which]
        for depth in upto:
            if depth == 0:
                for j in range(rows):
                    pltpu.make_async_copy(
                        ref.at[:, j, :], buf.at[ABOVE + j], load_sem.at[which, j]
                    ).wait()
                for t in range(SWEEPS):
                    span(levels[t], 1 + t, rows - 2 - 2 * t, 1)
                continue

            @pl.when(has_dn)
            def _(depth=depth):
                up_copy(which, depth - 1).wait_recv()

            if depth <= SWEEPS:

                @pl.when(has_up)
                def _(depth=depth):
                    dn_copy(which, depth - 1).wait_recv()

            for t in range(SWEEPS):
                low = 1 + t - depth
                high = rows - 2 - t + depth
                if depth <= SWEEPS:
                    span(levels[t], low, 2, high - low)
                else:
                    span(levels[t], high, 1, 1)

    sweeps(0, f0, f3, None, range(SWEEPS + 1))

    for j in range(rows):
        pltpu.make_async_copy(f3.at[j], field_ref.at[:, j, :], store_sem.at[j]).start()

    def read(j, total):
        value = jnp.zeros((fields, LANES), jnp.float32)
        for piece in split3(f3[j]):
            value = value + jnp.dot(piece, oh_t[...], preferred_element_type=jnp.float32)
        return total + jnp.where(cell_row == j, value, 0.0)

    got = lax.fori_loop(0, rows, read, jnp.zeros((fields, LANES), jnp.float32))
    got = got * coef_s[...]
    total = got[0:8]
    for c in range(1, chunks):
        total = total + got[8 * c : 8 * c + 8]
    total = total + pltpu.roll(total, 4, 0)
    for step in range(steps):
        parts[2 * step] = total
        copy = pltpu.make_async_remote_copy(
            src_ref=parts.at[2 * step],
            dst_ref=parts.at[2 * step + 1],
            send_sem=red_send.at[step],
            recv_sem=red_recv.at[step],
            device_id={"section": peer(step)},
        )
        copy.start()
        copy.wait()
        total = parts[2 * step] + parts[2 * step + 1]
    both = jnp.where(
        lane < 32, total + pltpu.roll(total, LANES - 32, 1), total + pltpu.roll(total, 32, 1)
    )
    pred_ref[...] = both[0:4, 0:32]
    obs = jnp.concatenate([obs_ref[...]] * 4, axis=1)
    obs = jnp.concatenate([obs] * 2, axis=0)
    miss = both - obs
    amp = coef_s[...] * jnp.concatenate([miss] * chunks, axis=0)
    pieces = split3(amp)
    for i in range(wide):
        keep = cell_row == i - (SWEEPS - 1)
        for p in range(3):
            lhs[p, i * fields : (i + 1) * fields, :] = jnp.where(
                keep, pieces[p], jnp.zeros_like(pieces[p])
            )

    def inject(i, _):
        at = pl.ds(pl.multiple_of(i * fields, fields), fields)
        value = jnp.zeros((fields, cols), jnp.float32)
        for p in range(3):
            value = value + jnp.dot(lhs[p, at, :], oh_e[...], preferred_element_type=jnp.float32)
        asrc[i] = value
        return 0

    lax.fori_loop(0, wide, inject, 0)

    def gradient(j):
        def body(c, acc):
            ks = pl.ds(pl.multiple_of(c * 8, 8), 8)
            f = f3[j, ks, :]
            a = a3[j, ks, :]
            fn = jnp.where(lane_c == cols - 1, 0.0, pltpu.roll(f, cols - 1, 1))
            an = jnp.where(lane_c == cols - 1, 0.0, pltpu.roll(a, cols - 1, 1))
            term = (f3[j + 1, ks, :] - f) * (a3[j + 1, ks, :] - a)
            term = term + (fn - f) * (an - a) + wcol_s[ks, 0:1] * (f * a)
            return acc + term

        acc = lax.fori_loop(0, chunks, body, jnp.zeros((8, cols), jnp.float32))
        return jnp.sum(acc, axis=0, keepdims=True) * (1.0 / srcs)

    sweeps(1, a0, a3, asrc, range(SWEEPS + 1))
    for j in range(rows - 1):
        if j == rows - 2:
            sweeps(0, f0, f3, None, (SWEEPS + 1,))
        grad_ref[j : j + 1, :] = gradient(j)
    sweeps(1, a0, a3, asrc, (SWEEPS + 1,))
    grad_ref[rows - 1 : rows, :] = gradient(rows - 1)

    @pl.when(has_up)
    def _():
        sig_copy(0).wait_send()
        for which, depth in order:
            up_copy(which, depth).wait_send()

    @pl.when(has_dn)
    def _():
        sig_copy(1).wait_send()
        for which, depth in order:
            if depth < SWEEPS:
                dn_copy(which, depth).wait_send()

    for j in range(rows):
        pltpu.make_async_copy(f3.at[j], field_ref.at[:, j, :], store_sem.at[j]).wait()


def solution(mesh):
    count = mesh.shape["section"]
    steps = count.bit_length() - 1

    def local(sigma, fwd, adj, src, rec, obs, wave, quad, off):
        kk, srcs, rows, cols = fwd.shape
        fields = kk * srcs
        deep = rows + ABOVE + BELOW
        wide = rows + 2 * SWEEPS - 1
        f32 = jnp.float32
        vmem = pl.BlockSpec(memory_space=pltpu.VMEM)
        anywhere = pl.BlockSpec(memory_space=pl.ANY)
        dma = pltpu.SemaphoreType.DMA
        grad, pred, field = pl.pallas_call(
            functools.partial(kernel, count, steps),
            out_shape=(
                jax.ShapeDtypeStruct((rows, cols), f32),
                jax.ShapeDtypeStruct(obs.shape, f32),
                jax.ShapeDtypeStruct((fields, rows, cols), f32),
            ),
            in_specs=[vmem, anywhere, anywhere] + [vmem] * 6,
            out_specs=(vmem, vmem, anywhere),
            scratch_shapes=[
                pltpu.VMEM((3 * rows, cols), f32),
                pltpu.VMEM((deep, fields, cols), f32),
                pltpu.VMEM((deep, fields, cols), f32),
                pltpu.VMEM((deep, fields, cols), f32),
                pltpu.VMEM((deep, fields, cols), f32),
                pltpu.VMEM((deep, fields, cols), f32),
                pltpu.VMEM((deep, fields, cols), f32),
                pltpu.VMEM((rows + 1, fields, cols), f32),
                pltpu.VMEM((rows + 1, fields, cols), f32),
                pltpu.VMEM((wide, fields, cols), f32),
                pltpu.VMEM((wide, 8, cols), f32),
                pltpu.VMEM((wide, fields, cols), f32),
                pltpu.VMEM((wide + 1, 8, cols), f32),
                pltpu.VMEM((wide, 8, cols), f32),
                pltpu.VMEM((wide, 8, cols), f32),
                pltpu.VMEM((fields, LANES), f32),
                pltpu.VMEM((fields, LANES), f32),
                pltpu.VMEM((LANES, cols), jnp.bfloat16),
                pltpu.VMEM((cols, LANES), jnp.bfloat16),
                pltpu.VMEM((3, wide * fields, LANES), jnp.bfloat16),
                pltpu.VMEM((2 * steps, 8, LANES), f32),
                dma((2,)),
                dma((2,)),
                dma((2, BELOW)),
                dma((2, BELOW)),
                dma((2, ABOVE)),
                dma((2, ABOVE)),
                dma((steps,)),
                dma((steps,)),
                dma((2, rows)),
                dma((rows,)),
            ],
            compiler_params=pltpu.CompilerParams(
                collective_id=0, has_side_effects=True, vmem_limit_bytes=48 << 20
            ),
        )(
            sigma,
            fwd.reshape(fields, rows, cols),
            adj.reshape(fields, rows, cols),
            src,
            rec,
            obs,
            wave.reshape(1, kk),
            quad.reshape(1, kk),
            off.reshape(1, off.shape[0]),
        )
        return grad, pred, field.reshape(fwd.shape)

    placed = (
        P(("line", "section"), None),
        P("line", None, "section", None),
        P("line", None, "section", None),
        P("line", None),
        P("line", None),
        P("line", None),
        P(),
        P(),
        P(),
    )
    return jax.shard_map(
        local,
        mesh=mesh,
        in_specs=placed,
        out_specs=(P(("line", "section"), None), P("line", None), P("line", None, "section", None)),
        check_vma=False,
    )
```

```python
import functools

import jax
import jax.numpy as jnp
from jax import lax
from jax.experimental import pallas as pl
from jax.experimental.pallas import tpu as pltpu
from jax.sharding import PartitionSpec as P

SWEEPS = 3
OMEGA = 0.8
CURRENT = 10.0
ABOVE = SWEEPS
BELOW = SWEEPS + 1
LANES = 128


def split3(value):
    high = value.astype(jnp.bfloat16)
    rest = value - high.astype(jnp.float32)
    mid = rest.astype(jnp.bfloat16)
    low = (rest - mid.astype(jnp.float32)).astype(jnp.bfloat16)
    return high, mid, low


def kernel(
    count,
    steps,
    sigma_ref,
    fwd_ref,
    adj_ref,
    src_ref,
    rec_ref,
    obs_ref,
    wave_ref,
    quad_ref,
    off_ref,
    grad_ref,
    pred_ref,
    field_ref,
    src_v,
    rec_v,
    obs_v,
    wave_v,
    quad_v,
    off_v,
    sig,
    f0,
    a0,
    t1,
    t2,
    b1,
    b2,
    f3,
    a3,
    rd,
    fsrc,
    asrc,
    face_v,
    face_l,
    face_r,
    coef_s,
    wcol_s,
    oh_e,
    oh_t,
    lhs,
    parts,
    sig_send,
    sig_recv,
    up_send,
    up_recv,
    dn_send,
    dn_recv,
    red_send,
    red_recv,
    load_sem,
    store_sem,
    small_sem,
):
    rows, cols = sigma_ref.shape
    fields = fwd_ref.shape[0]
    chunks = fields // 8
    wide = rows + 2 * SWEEPS - 1
    me = lax.axis_index("section")
    has_up = me > 0
    has_dn = me < count - 1
    start = me * rows

    def peer(step):
        bit = (me // (1 << step)) % 2
        return me + (1 - 2 * bit) * (1 << step)

    small = (
        (src_ref, src_v),
        (rec_ref, rec_v),
        (obs_ref, obs_v),
        (wave_ref, wave_v),
        (quad_ref, quad_v),
        (off_ref, off_v),
        (sigma_ref, sig.at[pl.ds(rows, rows)]),
    )
    for i, (ref, buf) in enumerate(small):
        pltpu.make_async_copy(ref, buf, small_sem.at[i]).start()

    for which, (ref, buf) in enumerate(((fwd_ref, f0), (adj_ref, a0))):
        for j in range(rows):
            pltpu.make_async_copy(
                ref.at[:, j, :], buf.at[ABOVE + j], load_sem.at[which, j]
            ).start()

    @pl.when(jnp.logical_not(has_up))
    def _():
        sig[0:rows, :] = jnp.zeros((rows, cols), jnp.float32)
        f0[0:ABOVE] = jnp.zeros((ABOVE, fields, cols), jnp.float32)
        a0[0:ABOVE] = jnp.zeros((ABOVE, fields, cols), jnp.float32)

    @pl.when(jnp.logical_not(has_dn))
    def _():
        sig[2 * rows : 3 * rows, :] = jnp.zeros((rows, cols), jnp.float32)
        f0[ABOVE + rows :] = jnp.zeros((BELOW, fields, cols), jnp.float32)
        a0[ABOVE + rows :] = jnp.zeros((BELOW, fields, cols), jnp.float32)

    barrier = pltpu.get_barrier_semaphore()

    @pl.when(has_up)
    def _():
        pl.semaphore_signal(barrier, inc=1, device_id={"section": me - 1})

    @pl.when(has_dn)
    def _():
        pl.semaphore_signal(barrier, inc=1, device_id={"section": me + 1})

    for step in range(steps):
        pl.semaphore_signal(barrier, inc=1, device_id={"section": peer(step)})

    beside = 2 - (count - me) // count - (me + 1) // count
    pl.semaphore_wait(barrier, steps + beside)

    def sig_copy(side):
        place = (2 * rows, 0)[side]
        return pltpu.make_async_remote_copy(
            src_ref=sigma_ref,
            dst_ref=sig.at[pl.ds(place, rows)],
            send_sem=sig_send.at[side],
            recv_sem=sig_recv.at[side],
            device_id={"section": (me - 1, me + 1)[side]},
        )

    def up_copy(which, depth):
        ref, buf = ((fwd_ref, f0), (adj_ref, a0))[which]
        return pltpu.make_async_remote_copy(
            src_ref=ref.at[:, depth, :],
            dst_ref=buf.at[ABOVE + rows + depth],
            send_sem=up_send.at[which, depth],
            recv_sem=up_recv.at[which, depth],
            device_id={"section": me - 1},
        )

    def dn_copy(which, depth):
        ref, buf = ((fwd_ref, f0), (adj_ref, a0))[which]
        return pltpu.make_async_remote_copy(
            src_ref=ref.at[:, rows - 1 - depth, :],
            dst_ref=buf.at[ABOVE - 1 - depth],
            send_sem=dn_send.at[which, depth],
            recv_sem=dn_recv.at[which, depth],
            device_id={"section": me + 1},
        )

    order = [(0, d) for d in range(SWEEPS)] + [(1, d) for d in range(SWEEPS)]
    order += [(0, SWEEPS), (1, SWEEPS)]

    @pl.when(has_up)
    def _():
        sig_copy(0).start()
        for which, depth in order:
            up_copy(which, depth).start()

    @pl.when(has_dn)
    def _():
        sig_copy(1).start()
        for which, depth in order:
            if depth < SWEEPS:
                dn_copy(which, depth).start()

    for i, (ref, buf) in enumerate(small):
        pltpu.make_async_copy(ref, buf, small_sem.at[i]).wait()

    lane = lax.broadcasted_iota(jnp.int32, (1, LANES), 1)
    rec = rec_v[...].astype(jnp.float32)
    rec_m = rec[0:1]
    rec_n = rec[1:2]
    none = jnp.full((1, LANES - 64), -1.0, jnp.float32)
    cell_f = jnp.concatenate([rec_m, rec_n, none], axis=1)
    cell = cell_f.astype(jnp.int32)
    cell_row = jnp.where(cell < 0, -1000, cell // cols - start)
    cell_col = jnp.where(cell < 0, -1, cell % cols)
    eye_e = lax.broadcasted_iota(jnp.int32, (LANES, LANES), 0) == lax.broadcasted_iota(
        jnp.int32, (LANES, LANES), 1
    )
    col_down = jnp.sum(
        jnp.where(eye_e, cell_col.astype(jnp.float32), 0.0), axis=1, keepdims=True
    ).astype(jnp.int32)
    oh_e[...] = jnp.where(
        lax.broadcasted_iota(jnp.int32, (LANES, cols), 1) == col_down, 1.0, 0.0
    ).astype(jnp.bfloat16)
    oh_t[...] = jnp.where(
        lax.broadcasted_iota(jnp.int32, (cols, LANES), 0) == cell_col, 1.0, 0.0
    ).astype(jnp.bfloat16)

    kk = wave_v.shape[1]
    srcs = fields // kk
    pick = lax.broadcasted_iota(jnp.int32, (fields, kk), 0) // srcs == lax.broadcasted_iota(
        jnp.int32, (fields, kk), 1
    )
    wave_col = jnp.sum(jnp.where(pick, wave_v[...], 0.0), axis=1, keepdims=True)
    quad_col = jnp.sum(jnp.where(pick, quad_v[...], 0.0), axis=1, keepdims=True)
    off = jnp.concatenate([off_v[...]] * 4, axis=1)
    sign = jnp.where(lane < 32, 1.0, jnp.where(lane < 64, -1.0, 0.0))
    coef_s[...] = quad_col * jnp.cos(wave_col * off) * sign
    wcol_s[...] = jnp.broadcast_to(wave_col * wave_col, (fields, LANES))


    @pl.when(has_dn)
    def _():
        sig_copy(0).wait_recv()

    @pl.when(has_up)
    def _():
        sig_copy(1).wait_recv()

    base = rows - (SWEEPS - 1)
    lane_c = lax.broadcasted_iota(jnp.int32, (8, cols), 1)
    own = lax.broadcasted_iota(jnp.int32, (8, srcs), 0) % srcs == lax.broadcasted_iota(
        jnp.int32, (8, srcs), 1
    )
    src = src_v[...].astype(jnp.float32)
    src_a = jnp.sum(jnp.where(own, src[0:1], 0.0), axis=1, keepdims=True).astype(jnp.int32)
    src_b = jnp.sum(jnp.where(own, src[1:2], 0.0), axis=1, keepdims=True).astype(jnp.int32)
    for i in range(wide):
        r = i - (SWEEPS - 1)
        centre = jnp.broadcast_to(sig[base + i : base + i + 1, :], (8, cols))
        above = jnp.broadcast_to(sig[base + i - 1 : base + i, :], (8, cols))
        below = jnp.broadcast_to(sig[base + i + 1 : base + i + 2, :], (8, cols))
        v_up = 0.5 * (centre + above)
        v_dn = 0.5 * (centre + below)
        left = jnp.where(lane_c == 0, 0.0, pltpu.roll(centre, 1, 1))
        right = jnp.where(lane_c == cols - 1, 0.0, pltpu.roll(centre, cols - 1, 1))
        h_l = 0.5 * (centre + left)
        h_r = 0.5 * (centre + right)
        face_v[i] = v_up
        if i == wide - 1:
            face_v[i + 1] = v_dn
        face_l[i] = jnp.where(lane_c == 0, 0.0, h_l)
        face_r[i] = jnp.where(lane_c == cols - 1, 0.0, h_r)
        around = v_up + v_dn + h_l + h_r
        flat = (start + r) * cols + lane_c
        fsrc[i] = jnp.where(flat == src_a, CURRENT, 0.0) + jnp.where(flat == src_b, -CURRENT, 0.0)
        inside = jnp.logical_and(start + r >= 0, start + r < count * rows)
        scale = jnp.where(inside, OMEGA, 0.0)
        safe = jnp.where(inside, 0.0, 1.0)

        def fill(c, _, i=i, around=around, centre=centre, scale=scale, safe=safe):
            ks = pl.ds(pl.multiple_of(c * 8, 8), 8)
            w2 = wcol_s[ks, 0:1]
            rd[i, ks, :] = scale / (around + w2 * centre + safe)
            return 0

        lax.fori_loop(0, chunks, fill, 0, unroll=True)

    def update(src, dst, shift, source, r):
        i = r + (SWEEPS - 1)

        def body(c, _):
            ks = pl.ds(pl.multiple_of(c * 8, 8), 8)
            u = src[r + ABOVE, ks, :]
            f = fsrc[i] if source is None else source[i, ks, :]
            acc = f + face_v[i] * src[r + ABOVE - 1, ks, :]
            acc = acc + face_v[i + 1] * src[r + ABOVE + 1, ks, :]
            acc = acc + face_l[i] * pltpu.roll(u, 1, 1)
            acc = acc + face_r[i] * pltpu.roll(u, cols - 1, 1)
            dst[r + shift, ks, :] = (1.0 - OMEGA) * u + acc * rd[i, ks, :]
            return 0

        lax.fori_loop(0, chunks, body, 0, unroll=True)

    def span(level, lo, number, stride):
        src, dst, shift, source = level

        def body(j, _):
            update(src, dst, shift, source, lo + j * stride)
            return 0

        lax.fori_loop(0, number, body, 0)

    def sweeps(which, first, last, source, upto):
        one, two = ((t1, t2), (b1, b2))[which]
        levels = (
            (first, one, ABOVE, source),
            (one, two, ABOVE, source),
            (two, last, 0, source),
        )
        ref, buf = ((fwd_ref, f0), (adj_ref, a0))[which]
        for depth in upto:
            if depth == 0:
                for j in range(rows):
                    pltpu.make_async_copy(
                        ref.at[:, j, :], buf.at[ABOVE + j], load_sem.at[which, j]
                    ).wait()
                for t in range(SWEEPS):
                    span(levels[t], 1 + t, rows - 2 - 2 * t, 1)
                continue

            @pl.when(has_dn)
            def _(depth=depth):
                up_copy(which, depth - 1).wait_recv()

            if depth <= SWEEPS:

                @pl.when(has_up)
                def _(depth=depth):
                    dn_copy(which, depth - 1).wait_recv()

            for t in range(SWEEPS):
                low = 1 + t - depth
                high = rows - 2 - t + depth
                if depth <= SWEEPS:
                    span(levels[t], low, 2, high - low)
                else:
                    span(levels[t], high, 1, 1)

    sweeps(0, f0, f3, None, range(SWEEPS + 1))

    for j in range(rows):
        pltpu.make_async_copy(f3.at[j], field_ref.at[:, j, :], store_sem.at[j]).start()

    def read(j, total):
        value = jnp.zeros((fields, LANES), jnp.float32)
        for piece in split3(f3[j]):
            value = value + jnp.dot(piece, oh_t[...], preferred_element_type=jnp.float32)
        return total + jnp.where(cell_row == j, value, 0.0)

    got = lax.fori_loop(0, rows, read, jnp.zeros((fields, LANES), jnp.float32))
    got = got * coef_s[...]
    total = got[0:8]
    for c in range(1, chunks):
        total = total + got[8 * c : 8 * c + 8]
    total = total + pltpu.roll(total, 4, 0)
    for step in range(steps):
        parts[2 * step] = total
        copy = pltpu.make_async_remote_copy(
            src_ref=parts.at[2 * step],
            dst_ref=parts.at[2 * step + 1],
            send_sem=red_send.at[step],
            recv_sem=red_recv.at[step],
            device_id={"section": peer(step)},
        )
        copy.start()
        copy.wait()
        total = parts[2 * step] + parts[2 * step + 1]
    both = jnp.where(
        lane < 32, total + pltpu.roll(total, LANES - 32, 1), total + pltpu.roll(total, 32, 1)
    )
    pred_ref[...] = both[0:4, 0:32]
    obs = jnp.concatenate([obs_v[...]] * 4, axis=1)
    obs = jnp.concatenate([obs] * 2, axis=0)
    miss = both - obs
    amp = coef_s[...] * jnp.concatenate([miss] * chunks, axis=0)
    pieces = split3(amp)
    for i in range(wide):
        keep = cell_row == i - (SWEEPS - 1)
        for p in range(3):
            lhs[p, i * fields : (i + 1) * fields, :] = jnp.where(
                keep, pieces[p], jnp.zeros_like(pieces[p])
            )

    def inject(i, _):
        at = pl.ds(pl.multiple_of(i * fields, fields), fields)
        value = jnp.zeros((fields, cols), jnp.float32)
        for p in range(3):
            value = value + jnp.dot(lhs[p, at, :], oh_e[...], preferred_element_type=jnp.float32)
        asrc[i] = value
        return 0

    lax.fori_loop(0, wide, inject, 0)

    def gradient(j):
        def body(c, acc):
            ks = pl.ds(pl.multiple_of(c * 8, 8), 8)
            f = f3[j, ks, :]
            a = a3[j, ks, :]
            fn = jnp.where(lane_c == cols - 1, 0.0, pltpu.roll(f, cols - 1, 1))
            an = jnp.where(lane_c == cols - 1, 0.0, pltpu.roll(a, cols - 1, 1))
            term = (f3[j + 1, ks, :] - f) * (a3[j + 1, ks, :] - a)
            term = term + (fn - f) * (an - a) + wcol_s[ks, 0:1] * (f * a)
            return acc + term

        acc = lax.fori_loop(0, chunks, body, jnp.zeros((8, cols), jnp.float32), unroll=True)
        return jnp.sum(acc, axis=0, keepdims=True) * (1.0 / srcs)

    sweeps(1, a0, a3, asrc, range(SWEEPS + 1))
    for j in range(rows - 1):
        if j == rows - 2:
            sweeps(0, f0, f3, None, (SWEEPS + 1,))
        grad_ref[j : j + 1, :] = gradient(j)
    sweeps(1, a0, a3, asrc, (SWEEPS + 1,))
    grad_ref[rows - 1 : rows, :] = gradient(rows - 1)

    @pl.when(has_up)
    def _():
        sig_copy(0).wait_send()
        for which, depth in order:
            up_copy(which, depth).wait_send()

    @pl.when(has_dn)
    def _():
        sig_copy(1).wait_send()
        for which, depth in order:
            if depth < SWEEPS:
                dn_copy(which, depth).wait_send()

    for j in range(rows):
        pltpu.make_async_copy(f3.at[j], field_ref.at[:, j, :], store_sem.at[j]).wait()


def solution(mesh):
    count = mesh.shape["section"]
    steps = count.bit_length() - 1

    def local(sigma, fwd, adj, src, rec, obs, wave, quad, off):
        kk, srcs, rows, cols = fwd.shape
        fields = kk * srcs
        deep = rows + ABOVE + BELOW
        wide = rows + 2 * SWEEPS - 1
        f32 = jnp.float32
        vmem = pl.BlockSpec(memory_space=pltpu.VMEM)
        anywhere = pl.BlockSpec(memory_space=pl.ANY)
        dma = pltpu.SemaphoreType.DMA
        grad, pred, field = pl.pallas_call(
            functools.partial(kernel, count, steps),
            out_shape=(
                jax.ShapeDtypeStruct((rows, cols), f32),
                jax.ShapeDtypeStruct(obs.shape, f32),
                jax.ShapeDtypeStruct((fields, rows, cols), f32),
            ),
            in_specs=[anywhere] * 9,
            out_specs=(vmem, vmem, anywhere),
            scratch_shapes=[
                pltpu.VMEM((2, src.shape[0]), jnp.int32),
                pltpu.VMEM((2, rec.shape[0]), jnp.int32),
                pltpu.VMEM(obs.shape, f32),
                pltpu.VMEM((1, kk), f32),
                pltpu.VMEM((1, kk), f32),
                pltpu.VMEM((1, off.shape[0]), f32),
                pltpu.VMEM((3 * rows, cols), f32),
                pltpu.VMEM((deep, fields, cols), f32),
                pltpu.VMEM((deep, fields, cols), f32),
                pltpu.VMEM((deep, fields, cols), f32),
                pltpu.VMEM((deep, fields, cols), f32),
                pltpu.VMEM((deep, fields, cols), f32),
                pltpu.VMEM((deep, fields, cols), f32),
                pltpu.VMEM((rows + 1, fields, cols), f32),
                pltpu.VMEM((rows + 1, fields, cols), f32),
                pltpu.VMEM((wide, fields, cols), f32),
                pltpu.VMEM((wide, 8, cols), f32),
                pltpu.VMEM((wide, fields, cols), f32),
                pltpu.VMEM((wide + 1, 8, cols), f32),
                pltpu.VMEM((wide, 8, cols), f32),
                pltpu.VMEM((wide, 8, cols), f32),
                pltpu.VMEM((fields, LANES), f32),
                pltpu.VMEM((fields, LANES), f32),
                pltpu.VMEM((LANES, cols), jnp.bfloat16),
                pltpu.VMEM((cols, LANES), jnp.bfloat16),
                pltpu.VMEM((3, wide * fields, LANES), jnp.bfloat16),
                pltpu.VMEM((2 * steps, 8, LANES), f32),
                dma((2,)),
                dma((2,)),
                dma((2, BELOW)),
                dma((2, BELOW)),
                dma((2, ABOVE)),
                dma((2, ABOVE)),
                dma((steps,)),
                dma((steps,)),
                dma((2, rows)),
                dma((rows,)),
                dma((7,)),
            ],
            compiler_params=pltpu.CompilerParams(
                collective_id=0, has_side_effects=True, vmem_limit_bytes=48 << 20
            ),
        )(
            sigma,
            fwd.reshape(fields, rows, cols),
            adj.reshape(fields, rows, cols),
            src.T,
            rec.T,
            obs,
            wave.reshape(1, kk),
            quad.reshape(1, kk),
            off.reshape(1, off.shape[0]),
        )
        return grad, pred, field.reshape(fwd.shape)

    placed = (
        P(("line", "section"), None),
        P("line", None, "section", None),
        P("line", None, "section", None),
        P("line", None),
        P("line", None),
        P("line", None),
        P(),
        P(),
        P(),
    )
    return jax.shard_map(
        local,
        mesh=mesh,
        in_specs=placed,
        out_specs=(P(("line", "section"), None), P("line", None), P("line", None, "section", None)),
        check_vma=False,
    )
```

```python
import functools

import jax
import jax.numpy as jnp
from jax import lax
from jax.experimental import pallas as pl
from jax.experimental.pallas import tpu as pltpu
from jax.sharding import PartitionSpec as P

SWEEPS = 3
OMEGA = 0.8
CURRENT = 10.0
ABOVE = SWEEPS
BELOW = SWEEPS + 1
LATER = (((1, 0),), ((1, 1),), ())
LAST = ((1, 2), (0, 3), (1, 3))
LANES = 128


def split3(value):
    high = value.astype(jnp.bfloat16)
    rest = value - high.astype(jnp.float32)
    mid = rest.astype(jnp.bfloat16)
    low = (rest - mid.astype(jnp.float32)).astype(jnp.bfloat16)
    return high, mid, low


def kernel(
    count,
    steps,
    sigma_ref,
    fwd_ref,
    adj_ref,
    src_ref,
    rec_ref,
    obs_ref,
    wave_ref,
    quad_ref,
    off_ref,
    grad_ref,
    pred_ref,
    field_ref,
    src_v,
    rec_v,
    obs_v,
    wave_v,
    quad_v,
    off_v,
    sig,
    f0,
    a0,
    t1,
    t2,
    b1,
    b2,
    f3,
    a3,
    rd,
    fsrc,
    asrc,
    face_v,
    face_l,
    face_r,
    coef_s,
    wcol_s,
    oh_e,
    oh_t,
    lhs,
    parts,
    sig_send,
    sig_recv,
    up_send,
    up_recv,
    dn_send,
    dn_recv,
    red_send,
    red_recv,
    load_sem,
    store_sem,
    small_sem,
):
    rows, cols = sigma_ref.shape
    fields = fwd_ref.shape[0]
    chunks = fields // 8
    wide = rows + 2 * SWEEPS - 1
    me = lax.axis_index("section")
    has_up = me > 0
    has_dn = me < count - 1
    start = me * rows

    def peer(step):
        bit = (me // (1 << step)) % 2
        return me + (1 - 2 * bit) * (1 << step)

    small = (
        (src_ref, src_v),
        (rec_ref, rec_v),
        (obs_ref, obs_v),
        (wave_ref, wave_v),
        (quad_ref, quad_v),
        (off_ref, off_v),
        (sigma_ref, sig.at[pl.ds(rows, rows)]),
    )
    for i, (ref, buf) in enumerate(small):
        pltpu.make_async_copy(ref, buf, small_sem.at[i]).start()

    for which, (ref, buf) in enumerate(((fwd_ref, f0), (adj_ref, a0))):
        for j in range(rows):
            pltpu.make_async_copy(
                ref.at[:, j, :], buf.at[ABOVE + j], load_sem.at[which, j]
            ).start()

    @pl.when(jnp.logical_not(has_up))
    def _():
        sig[0:rows, :] = jnp.zeros((rows, cols), jnp.float32)
        f0[0:ABOVE] = jnp.zeros((ABOVE, fields, cols), jnp.float32)
        a0[0:ABOVE] = jnp.zeros((ABOVE, fields, cols), jnp.float32)

    @pl.when(jnp.logical_not(has_dn))
    def _():
        sig[2 * rows : 3 * rows, :] = jnp.zeros((rows, cols), jnp.float32)
        f0[ABOVE + rows :] = jnp.zeros((BELOW, fields, cols), jnp.float32)
        a0[ABOVE + rows :] = jnp.zeros((BELOW, fields, cols), jnp.float32)

    barrier = pltpu.get_barrier_semaphore()

    @pl.when(has_up)
    def _():
        pl.semaphore_signal(barrier, inc=1, device_id={"section": me - 1})

    @pl.when(has_dn)
    def _():
        pl.semaphore_signal(barrier, inc=1, device_id={"section": me + 1})

    for step in range(steps):
        pl.semaphore_signal(barrier, inc=1, device_id={"section": peer(step)})

    beside = 2 - (count - me) // count - (me + 1) // count
    pl.semaphore_wait(barrier, steps + beside)

    def sig_copy(side):
        place = (2 * rows, 0)[side]
        return pltpu.make_async_remote_copy(
            src_ref=sigma_ref,
            dst_ref=sig.at[pl.ds(place, rows)],
            send_sem=sig_send.at[side],
            recv_sem=sig_recv.at[side],
            device_id={"section": (me - 1, me + 1)[side]},
        )

    def up_copy(which, depth):
        ref, buf = ((fwd_ref, f0), (adj_ref, a0))[which]
        return pltpu.make_async_remote_copy(
            src_ref=ref.at[:, depth, :],
            dst_ref=buf.at[ABOVE + rows + depth],
            send_sem=up_send.at[which, depth],
            recv_sem=up_recv.at[which, depth],
            device_id={"section": me - 1},
        )

    def dn_copy(which, depth):
        ref, buf = ((fwd_ref, f0), (adj_ref, a0))[which]
        return pltpu.make_async_remote_copy(
            src_ref=ref.at[:, rows - 1 - depth, :],
            dst_ref=buf.at[ABOVE - 1 - depth],
            send_sem=dn_send.at[which, depth],
            recv_sem=dn_recv.at[which, depth],
            device_id={"section": me + 1},
        )

    order = [(0, d) for d in range(SWEEPS)] + [(1, d) for d in range(SWEEPS)]
    order += [(0, SWEEPS), (1, SWEEPS)]

    @pl.when(has_up)
    def _():
        sig_copy(0).start()

    @pl.when(has_dn)
    def _():
        sig_copy(1).start()

    def send(pairs):
        @pl.when(has_up)
        def _():
            for which, depth in pairs:
                up_copy(which, depth).start()

        @pl.when(has_dn)
        def _():
            for which, depth in pairs:
                if depth < SWEEPS:
                    dn_copy(which, depth).start()

    send(order[:SWEEPS])

    for i, (ref, buf) in enumerate(small):
        pltpu.make_async_copy(ref, buf, small_sem.at[i]).wait()

    lane = lax.broadcasted_iota(jnp.int32, (1, LANES), 1)
    rec = rec_v[...].astype(jnp.float32)
    rec_m = rec[0:1]
    rec_n = rec[1:2]
    none = jnp.full((1, LANES - 64), -1.0, jnp.float32)
    cell_f = jnp.concatenate([rec_m, rec_n, none], axis=1)
    cell = cell_f.astype(jnp.int32)
    cell_row = jnp.where(cell < 0, -1000, cell // cols - start)
    cell_col = jnp.where(cell < 0, -1, cell % cols)
    eye_e = lax.broadcasted_iota(jnp.int32, (LANES, LANES), 0) == lax.broadcasted_iota(
        jnp.int32, (LANES, LANES), 1
    )
    col_down = jnp.sum(
        jnp.where(eye_e, cell_col.astype(jnp.float32), 0.0), axis=1, keepdims=True
    ).astype(jnp.int32)
    oh_e[...] = jnp.where(
        lax.broadcasted_iota(jnp.int32, (LANES, cols), 1) == col_down, 1.0, 0.0
    ).astype(jnp.bfloat16)
    oh_t[...] = jnp.where(
        lax.broadcasted_iota(jnp.int32, (cols, LANES), 0) == cell_col, 1.0, 0.0
    ).astype(jnp.bfloat16)

    kk = wave_v.shape[1]
    srcs = fields // kk
    pick = lax.broadcasted_iota(jnp.int32, (fields, kk), 0) // srcs == lax.broadcasted_iota(
        jnp.int32, (fields, kk), 1
    )
    wave_col = jnp.sum(jnp.where(pick, wave_v[...], 0.0), axis=1, keepdims=True)
    quad_col = jnp.sum(jnp.where(pick, quad_v[...], 0.0), axis=1, keepdims=True)
    off = jnp.concatenate([off_v[...]] * 4, axis=1)
    sign = jnp.where(lane < 32, 1.0, jnp.where(lane < 64, -1.0, 0.0))
    coef_s[...] = quad_col * jnp.cos(wave_col * off) * sign
    wcol_s[...] = jnp.broadcast_to(wave_col * wave_col, (fields, LANES))


    @pl.when(has_dn)
    def _():
        sig_copy(0).wait_recv()

    @pl.when(has_up)
    def _():
        sig_copy(1).wait_recv()

    base = rows - (SWEEPS - 1)
    lane_c = lax.broadcasted_iota(jnp.int32, (8, cols), 1)
    own = lax.broadcasted_iota(jnp.int32, (8, srcs), 0) % srcs == lax.broadcasted_iota(
        jnp.int32, (8, srcs), 1
    )
    src = src_v[...].astype(jnp.float32)
    src_a = jnp.sum(jnp.where(own, src[0:1], 0.0), axis=1, keepdims=True).astype(jnp.int32)
    src_b = jnp.sum(jnp.where(own, src[1:2], 0.0), axis=1, keepdims=True).astype(jnp.int32)
    for i in range(wide):
        r = i - (SWEEPS - 1)
        centre = jnp.broadcast_to(sig[base + i : base + i + 1, :], (8, cols))
        above = jnp.broadcast_to(sig[base + i - 1 : base + i, :], (8, cols))
        below = jnp.broadcast_to(sig[base + i + 1 : base + i + 2, :], (8, cols))
        v_up = 0.5 * (centre + above)
        v_dn = 0.5 * (centre + below)
        left = jnp.where(lane_c == 0, 0.0, pltpu.roll(centre, 1, 1))
        right = jnp.where(lane_c == cols - 1, 0.0, pltpu.roll(centre, cols - 1, 1))
        h_l = 0.5 * (centre + left)
        h_r = 0.5 * (centre + right)
        face_v[i] = v_up
        if i == wide - 1:
            face_v[i + 1] = v_dn
        face_l[i] = jnp.where(lane_c == 0, 0.0, h_l)
        face_r[i] = jnp.where(lane_c == cols - 1, 0.0, h_r)
        around = v_up + v_dn + h_l + h_r
        flat = (start + r) * cols + lane_c
        fsrc[i] = jnp.where(flat == src_a, CURRENT, 0.0) + jnp.where(flat == src_b, -CURRENT, 0.0)
        inside = jnp.logical_and(start + r >= 0, start + r < count * rows)
        scale = jnp.where(inside, OMEGA, 0.0)
        safe = jnp.where(inside, 0.0, 1.0)

        def fill(c, _, i=i, around=around, centre=centre, scale=scale, safe=safe):
            ks = pl.ds(pl.multiple_of(c * 8, 8), 8)
            w2 = wcol_s[ks, 0:1]
            rd[i, ks, :] = scale / (around + w2 * centre + safe)
            return 0

        lax.fori_loop(0, chunks, fill, 0, unroll=True)

    def update(src, dst, shift, source, r):
        i = r + (SWEEPS - 1)

        def body(c, _):
            ks = pl.ds(pl.multiple_of(c * 8, 8), 8)
            u = src[r + ABOVE, ks, :]
            f = fsrc[i] if source is None else source[i, ks, :]
            acc = f + face_v[i] * src[r + ABOVE - 1, ks, :]
            acc = acc + face_v[i + 1] * src[r + ABOVE + 1, ks, :]
            acc = acc + face_l[i] * pltpu.roll(u, 1, 1)
            acc = acc + face_r[i] * pltpu.roll(u, cols - 1, 1)
            dst[r + shift, ks, :] = (1.0 - OMEGA) * u + acc * rd[i, ks, :]
            return 0

        lax.fori_loop(0, chunks, body, 0, unroll=True)

    def span(level, lo, number, stride):
        src, dst, shift, source = level

        def body(j, _):
            update(src, dst, shift, source, lo + j * stride)
            return 0

        lax.fori_loop(0, number, body, 0)

    def sweeps(which, first, last, source, upto):
        one, two = ((t1, t2), (b1, b2))[which]
        levels = (
            (first, one, ABOVE, source),
            (one, two, ABOVE, source),
            (two, last, 0, source),
        )
        ref, buf = ((fwd_ref, f0), (adj_ref, a0))[which]
        for depth in upto:
            if depth == 0:
                for j in range(rows):
                    pltpu.make_async_copy(
                        ref.at[:, j, :], buf.at[ABOVE + j], load_sem.at[which, j]
                    ).wait()
                for t in range(SWEEPS):
                    span(levels[t], 1 + t, rows - 2 - 2 * t, 1)
                continue

            @pl.when(has_dn)
            def _(depth=depth):
                up_copy(which, depth - 1).wait_recv()

            if depth <= SWEEPS:

                @pl.when(has_up)
                def _(depth=depth):
                    dn_copy(which, depth - 1).wait_recv()

            if which == 0 and depth <= SWEEPS and LATER[depth - 1]:
                send(LATER[depth - 1])

            for t in range(SWEEPS):
                low = 1 + t - depth
                high = rows - 2 - t + depth
                if depth <= SWEEPS:
                    span(levels[t], low, 2, high - low)
                else:
                    span(levels[t], high, 1, 1)

    sweeps(0, f0, f3, None, range(SWEEPS + 1))

    for j in range(rows):
        pltpu.make_async_copy(f3.at[j], field_ref.at[:, j, :], store_sem.at[j]).start()

    def read(j, total):
        value = jnp.zeros((fields, LANES), jnp.float32)
        for piece in split3(f3[j]):
            value = value + jnp.dot(piece, oh_t[...], preferred_element_type=jnp.float32)
        return total + jnp.where(cell_row == j, value, 0.0)

    got = lax.fori_loop(0, rows, read, jnp.zeros((fields, LANES), jnp.float32))
    got = got * coef_s[...]
    total = got[0:8]
    for c in range(1, chunks):
        total = total + got[8 * c : 8 * c + 8]
    total = total + pltpu.roll(total, 4, 0)
    for step in range(steps):
        parts[2 * step] = total
        copy = pltpu.make_async_remote_copy(
            src_ref=parts.at[2 * step],
            dst_ref=parts.at[2 * step + 1],
            send_sem=red_send.at[step],
            recv_sem=red_recv.at[step],
            device_id={"section": peer(step)},
        )
        copy.start()
        copy.wait()
        total = parts[2 * step] + parts[2 * step + 1]
    send(LAST)
    both = jnp.where(
        lane < 32, total + pltpu.roll(total, LANES - 32, 1), total + pltpu.roll(total, 32, 1)
    )
    pred_ref[...] = both[0:4, 0:32]
    obs = jnp.concatenate([obs_v[...]] * 4, axis=1)
    obs = jnp.concatenate([obs] * 2, axis=0)
    miss = both - obs
    amp = coef_s[...] * jnp.concatenate([miss] * chunks, axis=0)
    pieces = split3(amp)
    for i in range(wide):
        keep = cell_row == i - (SWEEPS - 1)
        for p in range(3):
            lhs[p, i * fields : (i + 1) * fields, :] = jnp.where(
                keep, pieces[p], jnp.zeros_like(pieces[p])
            )

    def inject(i, _):
        at = pl.ds(pl.multiple_of(i * fields, fields), fields)
        value = jnp.zeros((fields, cols), jnp.float32)
        for p in range(3):
            value = value + jnp.dot(lhs[p, at, :], oh_e[...], preferred_element_type=jnp.float32)
        asrc[i] = value
        return 0

    lax.fori_loop(0, wide, inject, 0)

    def gradient(j):
        def body(c, acc):
            ks = pl.ds(pl.multiple_of(c * 8, 8), 8)
            f = f3[j, ks, :]
            a = a3[j, ks, :]
            fn = jnp.where(lane_c == cols - 1, 0.0, pltpu.roll(f, cols - 1, 1))
            an = jnp.where(lane_c == cols - 1, 0.0, pltpu.roll(a, cols - 1, 1))
            term = (f3[j + 1, ks, :] - f) * (a3[j + 1, ks, :] - a)
            term = term + (fn - f) * (an - a) + wcol_s[ks, 0:1] * (f * a)
            return acc + term

        acc = lax.fori_loop(0, chunks, body, jnp.zeros((8, cols), jnp.float32), unroll=True)
        return jnp.sum(acc, axis=0, keepdims=True) * (1.0 / srcs)

    sweeps(1, a0, a3, asrc, range(SWEEPS))
    for j in range(1, rows - 2):
        grad_ref[j : j + 1, :] = gradient(j)
    sweeps(1, a0, a3, asrc, (SWEEPS,))
    for j in (0, rows - 2):
        grad_ref[j : j + 1, :] = gradient(j)
    sweeps(0, f0, f3, None, (SWEEPS + 1,))
    sweeps(1, a0, a3, asrc, (SWEEPS + 1,))
    grad_ref[rows - 1 : rows, :] = gradient(rows - 1)

    @pl.when(has_up)
    def _():
        sig_copy(0).wait_send()
        for which, depth in order:
            up_copy(which, depth).wait_send()

    @pl.when(has_dn)
    def _():
        sig_copy(1).wait_send()
        for which, depth in order:
            if depth < SWEEPS:
                dn_copy(which, depth).wait_send()

    for j in range(rows):
        pltpu.make_async_copy(f3.at[j], field_ref.at[:, j, :], store_sem.at[j]).wait()


def solution(mesh):
    count = mesh.shape["section"]
    steps = count.bit_length() - 1

    def local(sigma, fwd, adj, src, rec, obs, wave, quad, off):
        kk, srcs, rows, cols = fwd.shape
        fields = kk * srcs
        deep = rows + ABOVE + BELOW
        wide = rows + 2 * SWEEPS - 1
        f32 = jnp.float32
        vmem = pl.BlockSpec(memory_space=pltpu.VMEM)
        anywhere = pl.BlockSpec(memory_space=pl.ANY)
        dma = pltpu.SemaphoreType.DMA
        grad, pred, field = pl.pallas_call(
            functools.partial(kernel, count, steps),
            out_shape=(
                jax.ShapeDtypeStruct((rows, cols), f32),
                jax.ShapeDtypeStruct(obs.shape, f32),
                jax.ShapeDtypeStruct((fields, rows, cols), f32),
            ),
            in_specs=[anywhere] * 9,
            out_specs=(vmem, vmem, anywhere),
            scratch_shapes=[
                pltpu.VMEM((2, src.shape[0]), jnp.int32),
                pltpu.VMEM((2, rec.shape[0]), jnp.int32),
                pltpu.VMEM(obs.shape, f32),
                pltpu.VMEM((1, kk), f32),
                pltpu.VMEM((1, kk), f32),
                pltpu.VMEM((1, off.shape[0]), f32),
                pltpu.VMEM((3 * rows, cols), f32),
                pltpu.VMEM((deep, fields, cols), f32),
                pltpu.VMEM((deep, fields, cols), f32),
                pltpu.VMEM((deep, fields, cols), f32),
                pltpu.VMEM((deep, fields, cols), f32),
                pltpu.VMEM((deep, fields, cols), f32),
                pltpu.VMEM((deep, fields, cols), f32),
                pltpu.VMEM((rows + 1, fields, cols), f32),
                pltpu.VMEM((rows + 1, fields, cols), f32),
                pltpu.VMEM((wide, fields, cols), f32),
                pltpu.VMEM((wide, 8, cols), f32),
                pltpu.VMEM((wide, fields, cols), f32),
                pltpu.VMEM((wide + 1, 8, cols), f32),
                pltpu.VMEM((wide, 8, cols), f32),
                pltpu.VMEM((wide, 8, cols), f32),
                pltpu.VMEM((fields, LANES), f32),
                pltpu.VMEM((fields, LANES), f32),
                pltpu.VMEM((LANES, cols), jnp.bfloat16),
                pltpu.VMEM((cols, LANES), jnp.bfloat16),
                pltpu.VMEM((3, wide * fields, LANES), jnp.bfloat16),
                pltpu.VMEM((2 * steps, 8, LANES), f32),
                dma((2,)),
                dma((2,)),
                dma((2, BELOW)),
                dma((2, BELOW)),
                dma((2, ABOVE)),
                dma((2, ABOVE)),
                dma((steps,)),
                dma((steps,)),
                dma((2, rows)),
                dma((rows,)),
                dma((7,)),
            ],
            compiler_params=pltpu.CompilerParams(
                collective_id=0, has_side_effects=True, vmem_limit_bytes=48 << 20
            ),
        )(
            sigma,
            fwd.reshape(fields, rows, cols),
            adj.reshape(fields, rows, cols),
            src.T,
            rec.T,
            obs,
            wave.reshape(1, kk),
            quad.reshape(1, kk),
            off.reshape(1, off.shape[0]),
        )
        return grad, pred, field.reshape(fwd.shape)

    placed = (
        P(("line", "section"), None),
        P("line", None, "section", None),
        P("line", None, "section", None),
        P("line", None),
        P("line", None),
        P("line", None),
        P(),
        P(),
        P(),
    )
    return jax.shard_map(
        local,
        mesh=mesh,
        in_specs=placed,
        out_specs=(P(("line", "section"), None), P("line", None), P("line", None, "section", None)),
        check_vma=False,
    )
```
